128 devices in a mesh: hst: 16 (over z, y_hi, core), local: 8 (over y_lo, x).
Axes of the slice: x: 4, y: 4 (y_hi: 2, y_lo: 2; y = y_hi * 2 + y_lo), z: 4, core: 2. Of those that a mesh axis runs over, the one named last changes fastest.
Arguments:
- pooled: bfloat16 [20480, 4096], P(('hst', 'local')), may hold values from -24 to 24
- cross_v: bfloat16 [512, 4096], replicated, may hold values from -0.09375 to 0.09375
- cross_u: bfloat16 [512, 4096], replicated, may hold values from -0.25 to 0.25
- cross_bias: float32 [4096], replicated, may hold values from -3 to 3
- head_weight: float32 [4096], replicated, may hold values from -0.09375 to 0.09375
- labels: int32 [20480], P(('hst', 'local')), may hold values from 0 to 1
- fn_weight: int32 [20480], P(('hst', 'local')), may hold values from 1 to 4
- row_ids: int32 [4, 32, 20480], P(None, 'hst'), may hold values from 0 to 8191
- bag_lengths: int32 [32, 20480], P('hst'), may hold values from 1 to 4
- table_rows: float32 [8192, 32, 128], P('local', 'hst'), may hold values from -6 to 6
- row_accum: float32 [8192, 32], P('local', 'hst'), may hold values from 0.0001 to 0.01
Outputs:
- grad_u: float32 [512, 4096], P(None, ('hst', 'local'))
- grad_v: float32 [512, 4096], P(None, ('hst', 'local'))
- grad_small: float32 [2, 4096], P(None, ('hst', 'local'))
- new_rows: float32 [8192, 32, 128], P('local', 'hst')
- new_accum: float32 [8192, 32], P('local', 'hst')
The draws below stay inside these ranges and needn't reach their ends.
Inputs may be any that keep to these rules, and one draw needn't show every extreme that they name: `row_ids`: a row of the feature's table.
All inputs are finite; a program needn't handle non-finite values.
Results may differ from the reference program's by a relative error of at most 0.003.
The reference program's roundings to bfloat16 on the way (of `hidden`, `scale_half`, `low_grad` and `input_grad`) count: a program that leaves them out, or rounds other values in their place, can miss the bound.
Values may be sent and summed in bfloat16 or wider, within the bound.
A program may use at most 128 MiB of HBM per device.

```python
import math
import jax
import jax.numpy as jnp
from jax import lax

NF = 32
E = 128
R = 512
POOL = 4
D = 4096
BATCH = 20480
ROWS = 8192


def set_ends(values, stream_key, low, top_value):
    longest = values.shape.index(max(values.shape))
    spots = []
    for shift in (0, 1):
        where = [jax.random.randint(jax.random.fold_in(stream_key, axis), (), 0, length) for axis, length in enumerate(values.shape)]
        where[longest] = (where[longest] + shift) % values.shape[longest]
        spots.append(tuple(where))
    return values.at[spots[0]].set(low).at[spots[1]].set(top_value)


def spiked(array, own_key, source, target, parts, factor):
    owner, partner = [(jnp.arange(array.shape[dim]) // (array.shape[dim] // parts)).reshape([-1 if axis == dim else 1 for axis in range(array.ndim)]) for dim in (source, target)]
    chosen = jax.random.permutation(own_key, parts)[partner]
    strong = (owner == chosen) | (owner == (partner + parts // 2) % parts)
    return jnp.where(strong, factor * array, array)


def steps_of(own_key, shape, cuts, low, largest):
    def one(axis_at, shards_of):
        steps = jax.random.uniform(jax.random.fold_in(jax.random.fold_in(own_key, 6), axis_at), (shards_of,), jnp.float32, low / len(cuts), largest / len(cuts))
        return jnp.repeat(jnp.exp(steps), shape[axis_at] // shards_of).reshape((-1,) + (1,) * (len(shape) - axis_at - 1))

    level = one(*cuts[0])
    for cut in cuts[1:]:
        level = level * one(*cut)
    return level


def normal_values(key, shape, width, reach, pieces=(), held_as=jnp.bfloat16):
    values = jax.random.normal(key, shape, jnp.float32) * width
    if len(pieces) > 0:
        values = steps_of(key, shape, pieces, -0.22, 0.18) * values
    return jnp.clip(values, min=-reach, max=reach).astype(held_as)


def bell_draw_with(rng, extent, spread, reach, shards, heavy, held_as=jnp.bfloat16):
    result = spread * jax.random.normal(rng, extent, jnp.float32)
    if shards:
        result = result * steps_of(rng, extent, shards, -0.22, 0.18)
    return jnp.clip(spiked(result, jax.random.fold_in(rng, 3), *heavy), -reach, reach).astype(held_as)


def setup_inputs(seed: int = 0) -> dict:
    key_list = jax.random.split(jax.random.key(seed), 12)
    return {
        "pooled": bell_draw_with(key_list[0], (BATCH, D), 1.0, 24.0, ((0, 128),), (0, 1, 128, 5.5)),
        "cross_v": normal_values(key_list[1], (R, D), D ** -0.5, 0.09375),
        "cross_u": normal_values(key_list[2], (R, D), R ** -0.5, 0.25),
        "cross_bias": normal_values(key_list[3], (D,), 0.5, 3.0, (), jnp.float32),
        "head_weight": normal_values(key_list[4], (D,), D ** -0.5, 0.09375, (), jnp.float32),
        "labels": set_ends(jax.random.randint(key_list[5], (BATCH,), 0, 2), jax.random.fold_in(key_list[5], 1), 0, 1).astype(jnp.int32),
        "fn_weight": set_ends(jax.random.randint(key_list[6], (BATCH,), 1, 5), jax.random.fold_in(key_list[6], 1), 1, 4).astype(jnp.int32),
        "row_ids": set_ends(jax.random.randint(key_list[7], (POOL, NF, BATCH), 0, ROWS), jax.random.fold_in(key_list[7], 1), 0, ROWS - 1).astype(jnp.int32),
        "bag_lengths": set_ends(jax.random.randint(key_list[8], (NF, BATCH), 1, POOL + 1), jax.random.fold_in(key_list[8], 1), 1, POOL).astype(jnp.int32),
        "table_rows": normal_values(key_list[9], (ROWS, NF, E), 1.0, 6.0, ((0, 8), (1, 16)), jnp.float32),
        "row_accum": jnp.clip(jnp.exp(math.log(0.01) - 4.6051702 * jax.random.uniform(key_list[10], (ROWS, NF), jnp.float32) ** steps_of(key_list[10], (ROWS, NF), ((0, 8), (1, 16)), -0.2, 0.2)), 0.0001, 0.01),
    }


learn_rate = 0.05
epsilon = 1e-08

def reference(pooled, cross_v, cross_u, cross_bias, head_weight, labels, fn_weight, row_ids, bag_lengths, table_rows, row_accum):
    hidden = lax.dot_general(pooled, cross_v, (((1,), (1,)), ((), ())), preferred_element_type=jnp.float32).astype(jnp.bfloat16)
    scale = jnp.dot(hidden, cross_u, preferred_element_type=jnp.float32) + cross_bias
    features = pooled.astype(jnp.float32)
    mixed = features * scale + features
    logits = lax.optimization_barrier(jnp.sum(mixed * head_weight, axis=1))
    chance = jax.nn.sigmoid(logits)
    logit_grad = fn_weight.astype(jnp.float32) * (chance - labels.astype(jnp.float32))
    out_grad = logit_grad[:, None] * head_weight
    scale_grad = out_grad * features
    scale_half = scale_grad.astype(jnp.bfloat16)
    grad_u = lax.dot_general(hidden, scale_half, (((0,), (0,)), ((), ())), preferred_element_type=jnp.float32)
    low_grad = lax.dot_general(scale_half, cross_u, (((1,), (1,)), ((), ())), preferred_element_type=jnp.float32).astype(jnp.bfloat16)
    grad_v = lax.dot_general(low_grad, pooled, (((0,), (0,)), ((), ())), preferred_element_type=jnp.float32)
    grad_small = jnp.stack([lax.optimization_barrier(jnp.sum(scale_grad, axis=0)), lax.optimization_barrier(jnp.sum(logit_grad[:, None] * mixed, axis=0))])
    input_grad = (out_grad * (scale + 1.0) + jnp.dot(low_grad, cross_v, preferred_element_type=jnp.float32)).astype(jnp.bfloat16)
    values = input_grad.reshape(BATCH * NF, E).astype(jnp.float32)
    feature_col = jnp.arange(NF, dtype=jnp.int32)[:, None]
    row_grad = jnp.zeros((ROWS * NF, E), jnp.float32)
    for slot in range(POOL):
        live = slot < bag_lengths
        segment = jnp.where(live, row_ids[slot] * NF + feature_col, ROWS * NF).astype(jnp.int32)
        segment = segment.T.reshape(-1)
        row_grad = row_grad + jax.ops.segment_sum(values, segment, num_segments=ROWS * NF + 1)[:-1]
    row_grad = row_grad.reshape(ROWS, NF, E)
    new_accum = row_accum + lax.optimization_barrier(jnp.mean(row_grad * row_grad, axis=2))
    new_rows = table_rows - learn_rate * row_grad / (jnp.sqrt(new_accum)[:, :, None] + epsilon)
    return (grad_u, grad_v, grad_small, new_rows, new_accum)
```

```python
import jax
import jax.numpy as jnp
from jax import lax
from jax.experimental import pallas as pl
from jax.experimental.pallas import tpu as pltpu
from jax.sharding import PartitionSpec as P

learn_rate = 0.05
epsilon = 1e-08
MESH = pl.DeviceIdType.MESH
F32 = jnp.float32
BF16 = jnp.bfloat16

B = 160
R = 512
D = 4096
W = 256
G = 8
KC = G * B
RC = 1024
NT = (((1,), (1,)), ((), ()))
TN = (((0,), (0,)), ((), ()))

GROUP = [(2, 0), (2, 1), (1, 0), (3, 0), (1, 1), (3, 1), (0, 1), (0, 0)]
PLANE = [(kx, ka, kb) for kx in (2, 1, 3, 0) for ka in (1, 0) for kb in (1, 0)]


def kernel(
    pooled, v_hbm, u_hbm, bias, head, labels, fn_weight, ids,
    dense_out, small_out, rows_out,
    pool_v, v_v, u_v, scale_v, target, weight,
    pool_g, hid_g, low_g, lg_g, small_s, small_g,
    ig_s, e1, gath, half_g,
    dense_s, dense_r, tsmall_s, tsmall_r,
    acc, x_s, x_r,
    loc_sem, pg_s, pg_r, hg_s, hg_r, lo_s, lo_r, lg_s, lg_r, sm_s, sm_r,
    z_s, z_r, y_s, y_r, dn_s, dn_r, ts_s, ts_r, xs_s, xs_r,
):
    h = lax.axis_index("hst")
    l = lax.axis_index("local")
    z, yh, c = h // 4, (h // 2) % 2, h % 2
    yl, x = l // 4, l % 4
    me = z * 2 + c

    def group_dev(kz, kc):
        zz, cc = (z + kz) % 4, (c + kc) % 2
        return (zz * 4 + yh * 2 + cc, l), zz * 2 + cc

    def plane_dev(kx, ka, kb):
        hh, bb, xx = (yh + ka) % 2, (yl + kb) % 2, (x + kx) % 4
        return (z * 4 + hh * 2 + c, bb * 4 + xx), hh * W + (bb * 4 + xx) * 32

    def rcopy(src, dst, ss, rs, dev):
        return pltpu.make_async_remote_copy(
            src_ref=src, dst_ref=dst, send_sem=ss, recv_sem=rs, device_id=dev, device_id_type=MESH
        )

    barrier = pltpu.get_barrier_semaphore()
    for off in GROUP[:-1]:
        pl.semaphore_signal(barrier, inc=1, device_id=group_dev(*off)[0], device_id_type=MESH)
    for off in PLANE[:-1]:
        pl.semaphore_signal(barrier, inc=1, device_id=plane_dev(*off)[0], device_id_type=MESH)

    loads = [
        pltpu.make_async_copy(pooled, pool_v, loc_sem.at[0]),
        pltpu.make_async_copy(v_hbm, v_v, loc_sem.at[1]),
        pltpu.make_async_copy(u_hbm, u_v, loc_sem.at[2]),
    ]
    for ld in loads:
        ld.start()

    lane = lax.broadcasted_iota(jnp.int32, (8, 640), 1)
    for ys in range(4):
        for g in range(2):
            out = jnp.zeros((8, 640), jnp.int32)
            for i in range(4):
                hs = (2 * g + i // 2) * 4 + (ys // 2) * 2 + i % 2
                win = ids[:, pl.ds(hs * 1280 + (ys % 2) * 640, 640)]
                win = pltpu.roll(win, (160 * i + 640 - 160 * x) % 640, 1)
                out = jnp.where((lane >= 160 * i) & (lane < 160 * (i + 1)), win, out)
            target[:, pl.ds((ys * 2 + g) * 640, 640)] = out.astype(F32)
    for f in range(2):
        t = [target[pl.ds(f * 4 + s, 1), :] for s in range(4)]
        e01, e02, e03 = t[0] == t[1], t[0] == t[2], t[0] == t[3]
        e12, e13, e23 = t[1] == t[2], t[1] == t[3], t[2] == t[3]
        one = lambda m: jnp.where(m, 1.0, 0.0)
        weight[pl.ds(f * 4, 1), :] = 1.0 + one(e01) + one(e02) + one(e03)
        weight[pl.ds(f * 4 + 1, 1), :] = 1.0 + one(e12) + one(e13)
        weight[pl.ds(f * 4 + 2, 1), :] = 1.0 + one(e23)
        weight[pl.ds(f * 4 + 3, 1), :] = jnp.ones_like(t[0])
        target[pl.ds(f * 4 + 1, 1), :] = jnp.where(e01, -1.0, t[1])
        target[pl.ds(f * 4 + 2, 1), :] = jnp.where(e02 | e12, -1.0, t[2])
        target[pl.ds(f * 4 + 3, 1), :] = jnp.where(e03 | e13 | e23, -1.0, t[3])

    pl.semaphore_wait(barrier, len(GROUP) + len(PLANE) - 2)

    sends = []

    def go(copy):
        copy.start()
        sends.append(copy)
        return copy

    pg = []
    for k, off in enumerate(GROUP[:-1]):
        dev, m = group_dev(*off)
        for b in range(2):
            col = pl.multiple_of(((m // 2) * 4 + b * 2 + m % 2) * W, W)
            pg.append(go(rcopy(pooled.at[:, pl.ds(col, W)], pool_g.at[k, :, pl.ds(b * W, W)],
                               pg_s.at[k * 2 + b], pg_r.at[k * 2 + b], dev)))

    loads[0].wait()
    loads[1].wait()
    hid = lax.dot_general(pool_v[...], v_v[...], NT, preferred_element_type=F32).astype(BF16)
    hid_g[7] = hid
    hg = [go(rcopy(hid_g.at[7], hid_g.at[k], hg_s.at[k], hg_r.at[k], group_dev(*off)[0]))
          for k, off in enumerate(GROUP[:-1])]
    loads[2].wait()

    part = jnp.zeros((B, 128), F32)
    for j in range(8):
        cols = pl.ds(j * 512, 512)
        sc = jnp.dot(hid_g[7], u_v[:, cols], preferred_element_type=F32) + bias[:, cols]
        scale_v[:, cols] = sc
        f = pool_v[:, cols].astype(F32)
        prod = (f * sc + f) * head[:, cols]
        part = part + (prod[:, 0:128] + prod[:, 128:256]) + (prod[:, 256:384] + prod[:, 384:512])
    logits = jnp.sum(part, axis=1, keepdims=True)
    chance = 1.0 / (1.0 + jnp.exp(-logits))
    lg = fn_weight[...] * (chance - labels[...])
    lgb = jnp.broadcast_to(lg, (B, 128))
    lg_g[7] = lgb
    lgc = [go(rcopy(lg_g.at[7], lg_g.at[k], lg_s.at[k], lg_r.at[k], group_dev(*off)[0]))
           for k, off in enumerate(GROUP[:-1])]
    lgw = jnp.concatenate([lgb, lgb], axis=1)

    low = jnp.zeros((B, R), F32)
    for j in range(16):
        cols = pl.ds(j * W, W)
        f = pool_v[:, cols].astype(F32)
        sg = (lgw * head[:, cols]) * f
        low = low + lax.dot_general(sg.astype(BF16), u_v[:, cols], NT, preferred_element_type=F32)
        mixed = f * scale_v[:, cols] + f
        m, b = (j // 4) * 2 + j % 2, (j // 2) % 2
        small_s[m, b] = jnp.concatenate(
            [jnp.sum(sg, axis=0, keepdims=True), jnp.sum(lgw * mixed, axis=0, keepdims=True),
             jnp.zeros((6, W), F32)], axis=0)
    low_g[7] = low.astype(BF16)

    zc = []
    for k, off in enumerate(GROUP):
        dev, m = group_dev(*off)
        for b in range(2):
            cols = pl.ds(pl.multiple_of(((m // 2) * 4 + b * 2 + m % 2) * W, W), W)
            ig = (lgw * head[:, cols]) * (scale_v[:, cols] + 1.0) + jnp.dot(
                low_g[7], v_v[:, cols], preferred_element_type=F32)
            if k < 7:
                ig_s[k, b] = ig.astype(BF16)
            else:
                e1[me, b] = ig.astype(BF16)
        if k < 7:
            zc.append(go(rcopy(ig_s.at[k], e1.at[me], z_s.at[k], z_r.at[k], dev)))
    loc = [go(rcopy(low_g.at[7], low_g.at[k], lo_s.at[k], lo_r.at[k], group_dev(*off)[0]))
           for k, off in enumerate(GROUP[:-1])]
    smc = []
    for k, off in enumerate(GROUP[:-1]):
        dev, m = group_dev(*off)
        smc.append(go(rcopy(small_s.at[m], small_g.at[k], sm_s.at[k], sm_r.at[k], dev)))

    for cp in pg:
        cp.wait_recv()
    for b in range(2):
        col = pl.multiple_of(h // 4 * 4 * W + b * 2 * W + c * W, W)
        pool_g[7, :, pl.ds(b * W, W)] = pool_v[:, pl.ds(col, W)]
    for cp in lgc + hg:
        cp.wait_recv()
    for k in range(8):
        for b in range(2):
            col = pl.multiple_of(h // 4 * 4 * W + b * 2 * W + c * W, W)
            lgk = jnp.concatenate([lg_g[k], lg_g[k]], axis=1)
            half_g[pl.ds(k * B, B), pl.ds(b * W, W)] = (
                (lgk * head[:, pl.ds(col, W)]) * pool_g[k, :, pl.ds(b * W, W)].astype(F32)
            ).astype(BF16)
    dense_s[:, pl.ds(0, R)] = lax.dot_general(
        half_g[...], hid_g[...].reshape(KC, R), TN, preferred_element_type=F32).astype(BF16)

    yc = []

    def forward(src_m, j):
        gath[0, src_m] = e1[src_m, yh]
        for d in (1, 2, 3):
            ka, kb = d // 2, d % 2
            b = yh if ka == 0 else 1 - yh
            yc.append(go(rcopy(e1.at[src_m, b], gath.at[d, src_m], y_s.at[d - 1, j], y_r.at[d - 1, j],
                               plane_dev(0, ka, kb)[0])))

    forward(me, 7)
    for k in (6, 2, 3, 4, 5, 0, 1):
        zc[k].wait_recv()
        kz, kc = GROUP[k]
        forward(((z - kz + 4) % 4) * 2 + (c + kc) % 2, k)

    for cp in loc + smc:
        cp.wait_recv()
    dense_s[:, pl.ds(R, R)] = lax.dot_general(
        pool_g[...].reshape(KC, R), low_g[...].reshape(KC, R), TN, preferred_element_type=F32).astype(BF16)
    for b in range(2):
        tot = small_s[me, b]
        for k in range(7):
            tot = tot + small_g[k, b]
        tsmall_s[pl.ds(b * W, W), :] = jnp.concatenate([tot, jnp.zeros((120, W), F32)], axis=0).T
    dnc, tsc = [], []
    for k, off in enumerate(PLANE[:-1]):
        dev, row = plane_dev(*off)
        row = pl.multiple_of(row, 32)
        dnc.append(go(rcopy(dense_s.at[pl.ds(row, 32)], dense_r.at[k], dn_s.at[k], dn_r.at[k], dev)))
        tsc.append(go(rcopy(tsmall_s.at[pl.ds(row, 32)], tsmall_r.at[k], ts_s.at[k], ts_r.at[k], dev)))

    iota = lax.broadcasted_iota(jnp.int32, (16, KC), 0).astype(F32).astype(BF16)
    acc[...] = jnp.zeros_like(acc)

    def x_copy(kx):
        return rcopy(x_s.at[kx], x_r.at[kx], xs_s.at[kx], xs_r.at[kx], (h, yl * 4 + (x + kx + 1) % 4))

    def y_step(d, carry):
        @pl.when(d > 0)
        def _():
            def one_wait(j, cc):
                rcopy(e1.at[j, 0], gath.at[d, j], y_s.at[d - 1, j], y_r.at[d - 1, j], (h, l)).wait_recv()
                return cc
            lax.fori_loop(0, 8, one_wait, 0)

        src = ((yh + d // 2) % 2) * 2 + (yl + d % 2) % 2
        lanes = pl.ds(pl.multiple_of(src * KC, 128), KC)

        def chunk_step(kx, cc):
            base = (yl * 4 + (x + kx + 1) % 4) * RC
            for f in range(2):
                tt = [target[pl.ds(f * 4 + s, 1), lanes] for s in range(4)]
                ws = [jnp.broadcast_to(weight[pl.ds(f * 4 + s, 1), lanes], (16, KC)).astype(BF16)
                      for s in range(4)]
                tiles = []
                for sb in range(RC // 256):
                    low_row = (base + sb * 256).astype(F32)
                    ts = [jnp.broadcast_to(tt[s] - low_row, (16, KC)).astype(BF16) for s in range(4)]
                    for i in range(16):
                        it = iota + jnp.asarray(16 * i, BF16)
                        cnt = jnp.zeros((16, KC), BF16)
                        for s in range(4):
                            cnt = jnp.where(it == ts[s], ws[s], cnt)
                        tiles.append(cnt)
                counts = jnp.concatenate(tiles, axis=0)
                g = gath[d, :, :, pl.ds(f * 128, 128)].reshape(KC, 128)
                acc[kx, :, pl.ds(f * 128, 128)] += jnp.dot(counts, g, preferred_element_type=F32)

            @pl.when((d == 3) & (kx < 3))
            def _():
                x_s[kx] = acc[kx].astype(BF16)
                x_copy(kx).start()
            return cc

        return lax.fori_loop(0, 4, chunk_step, carry)

    lax.fori_loop(0, 4, y_step, 0)

    for cp in dnc + tsc:
        cp.wait_recv()
    dev, row = plane_dev(*PLANE[-1])
    row = pl.multiple_of(row, 32)
    tot = dense_s[pl.ds(row, 32)].astype(F32)
    small = tsmall_s[pl.ds(row, 32)]
    for k in range(15):
        tot = tot + dense_r[k].astype(F32)
        small = small + tsmall_r[k]
    dense_out[...] = tot
    small_out[...] = small

    for kx in range(3):
        x_copy(kx).wait_recv()
    rows_out[...] = acc[3] + (x_r[0].astype(F32) + x_r[1].astype(F32)) + x_r[2].astype(F32)
    for kx in range(3):
        x_copy(kx).wait_send()
    for cp in sends:
        cp.wait_send()


def fused(pooled, cross_v, cross_u, bias, head, labels, fn_weight, ids):
    any_, vmem = pl.BlockSpec(memory_space=pl.ANY), pl.BlockSpec(memory_space=pltpu.VMEM)
    V, S = pltpu.VMEM, lambda *n: pltpu.SemaphoreType.DMA(n)
    return pl.pallas_call(
        kernel,
        out_shape=(
            jax.ShapeDtypeStruct((32, 2 * R), F32),
            jax.ShapeDtypeStruct((32, 128), F32),
            jax.ShapeDtypeStruct((RC, W), F32),
        ),
        in_specs=[any_, any_, any_, vmem, vmem, vmem, vmem, vmem],
        out_specs=(vmem, vmem, vmem),
        scratch_shapes=[
            V((B, D), BF16), V((R, D), BF16), V((R, D), BF16), V((B, D), F32),
            V((8, 4 * KC), F32), V((8, 4 * KC), F32),
            V((G, B, R), BF16), V((G, B, R), BF16), V((G, B, R), BF16), V((G, B, 128), F32),
            V((G, 2, 8, W), F32), V((G, 2, 8, W), F32),
            V((G - 1, 2, B, W), BF16), V((G, 2, B, W), BF16), V((4, G, B, W), BF16), V((KC, R), BF16),
            V((R, 2 * R), BF16), V((15, 32, 2 * R), BF16), V((R, 128), F32), V((15, 32, 128), F32),
            V((4, RC, W), F32), V((3, RC, W), BF16), V((3, RC, W), BF16),
            S(3), S(14), S(14), S(7), S(7), S(7), S(7), S(7), S(7), S(7), S(7),
            S(7), S(7), S(3, 8), S(3, 8), S(15), S(15), S(15), S(15), S(3), S(3),
        ],
        compiler_params=pltpu.CompilerParams(
            collective_id=0, has_side_effects=True, vmem_limit_bytes=58 * 2**20
        ),
        cost_estimate=pl.CostEstimate(flops=16 * 10**9, bytes_accessed=12 * 10**6, transcendentals=160),
    )(pooled, cross_v, cross_u, bias, head, labels, fn_weight, ids)


def body(
    pooled, cross_v, cross_u, cross_bias, head_weight, labels, fn_weight,
    row_ids, bag_lengths, table_rows, row_accum,
):
    slot = lax.broadcasted_iota(jnp.int32, row_ids.shape, 0)
    live = jnp.where(slot < bag_lengths[None], row_ids, -1)
    ids = live.transpose(1, 0, 2).reshape(8, -1)
    dense, small, row_grad = fused(
        pooled, cross_v, cross_u, cross_bias[None], head_weight[None],
        labels.astype(F32)[:, None], fn_weight.astype(F32)[:, None], ids,
    )
    row_grad = row_grad.reshape(RC, 2, 128)
    new_accum = row_accum + jnp.mean(row_grad * row_grad, axis=2)
    new_rows = table_rows - learn_rate * row_grad / (jnp.sqrt(new_accum)[:, :, None] + epsilon)
    return (dense[:, :R].T, dense[:, R:].T, small[:, :2].T, new_rows, new_accum)


def solution(mesh):
    placed = (
        P(("hst", "local"), None), P(), P(), P(), P(), P(("hst", "local")), P(("hst", "local")),
        P(None, "hst", None), P("hst", None), P("local", "hst", None), P("local", "hst"),
    )
    both = P(None, ("hst", "local"))
    return jax.shard_map(
        body, mesh=mesh, in_specs=placed,
        out_specs=(both, both, both, P("local", "hst", None), P("local", "hst")),
        check_vma=False,
    )
```

```python
import jax
import jax.numpy as jnp
from jax import lax
from jax.experimental import pallas as pl
from jax.experimental.pallas import tpu as pltpu
from jax.sharding import PartitionSpec as P

learn_rate = 0.05
epsilon = 1e-08
MESH = pl.DeviceIdType.MESH
F32 = jnp.float32
BF16 = jnp.bfloat16

B = 160
R = 512
D = 4096
W = 256
E = 128
G = 8
KC = G * B
RC = 1024
NT = (((1,), (1,)), ((), ()))
TN = (((0,), (0,)), ((), ()))

GROUP = [(2, 0), (2, 1), (1, 0), (3, 0), (1, 1), (3, 1), (0, 1)]
ARRIVE = [(0, 1), (1, 0), (3, 0), (1, 1), (3, 1), (2, 0), (2, 1)]
YS = [(0, 1), (1, 0), (1, 1)]
DENSE = [(2, 0), (2, 1), (1, 0), (3, 0), (1, 1), (3, 1), (0, 1)]


def kernel(
    pooled, v_hbm, u_hbm, bias, head, labels, fn_weight, ids_hbm, lens_hbm, table_hbm, accum,
    out_u, out_v, out_small, out_rows, out_accum,
    pool_v, v_v, u_v, scale_v, ids, lens, table, target, weight, cols_v,
    pool_g, hid_g, low_g, lg_g, small_s, small_g,
    ig_s, e1, gath, half_g,
    dense_s, dense_r, tsmall_s, tsmall_r, d2_s, d2_r, d3_r,
    acc, x_s, x_r,
    loc_sem, pg_s, pg_r, hg_s, hg_r, lo_s, lo_r, lg_s, lg_r, sm_s, sm_r,
    z_s, z_r, y1_s, y1_r, y3_s, y3_r, y2_s, y2_r, dn_s, dn_r, ts_s, ts_r, d2_ss, d2_rs, d3_ss, d3_rs, xs_s, xs_r,
):
    h = lax.axis_index("hst")
    l = lax.axis_index("local")
    z, yh, c = h // 4, (h // 2) % 2, h % 2
    yl, x = l // 4, l % 4
    me = z * 2 + c

    def group_dev(kz, kc):
        zz, cc = (z + kz) % 4, (c + kc) % 2
        return (zz * 4 + yh * 2 + cc, l), zz * 2 + cc

    def y_dev(ka, kb):
        return (z * 4 + ((yh + ka) % 2) * 2 + c, ((yl + kb) % 2) * 4 + x)

    def x_dev(kx):
        return (h, yl * 4 + (x + kx) % 4)

    def dense_dev(kx, kc):
        xx, cc = (x + kx) % 4, (c + kc) % 2
        return (z * 4 + yh * 2 + cc, yl * 4 + xx), xx * 2 + cc

    def dense_cols(m, zt):
        col = (zt * 4 + (m // 4) * 2 + m % 2) * W + ((m // 2) % 2) * E
        return pl.ds(pl.multiple_of(col, E), E)

    def rcopy(src, dst, ss, rs, dev):
        return pltpu.make_async_remote_copy(
            src_ref=src, dst_ref=dst, send_sem=ss, recv_sem=rs, device_id=dev, device_id_type=MESH
        )

    def src_of(kz, kc):
        return ((z - kz + 4) % 4) * 2 + (c + kc) % 2

    barrier = pltpu.get_barrier_semaphore()
    partners = [group_dev(*o)[0] for o in GROUP] + [y_dev(*o) for o in YS] + [dense_dev(*o)[0] for o in DENSE[:-1]]
    for dev in partners:
        pl.semaphore_signal(barrier, inc=1, device_id=dev, device_id_type=MESH)

    def load(src, dst, i):
        cp = pltpu.make_async_copy(src, dst, loc_sem.at[i])
        cp.start()
        return cp

    ld_ids, ld_lens = load(ids_hbm, ids, 0), load(lens_hbm, lens, 1)
    ld_pool, ld_v, ld_u = load(pooled, pool_v, 2), load(v_hbm, v_v, 3), load(u_hbm, u_v, 4)
    ld_table = load(table_hbm, table, 5)

    cols_v[...] = jnp.zeros_like(cols_v)
    cols_v[pl.ds(0, 1), pl.ds(0, B)] = labels[...].astype(F32)
    cols_v[pl.ds(1, 1), pl.ds(0, B)] = fn_weight[...].astype(F32)

    def column(row):
        return jnp.broadcast_to(row, (128, row.shape[1])).T

    lab_c = column(cols_v[pl.ds(0, 1), :])[:B]
    fnw_c = column(cols_v[pl.ds(1, 1), :])[:B]

    pl.semaphore_wait(barrier, len(partners))

    sends = []

    def go(copy):
        copy.start()
        sends.append(copy)
        return copy

    pg = []
    for k, (kx, kc) in enumerate(DENSE):
        dev, m = dense_dev(kx, kc)
        for zt in range(4):
            pg.append(go(rcopy(pooled.at[:, dense_cols(m, zt)], pool_g.at[kc * 4 + kx, :, pl.ds(zt * E, E)],
                               pg_s.at[k * 4 + zt], pg_r.at[k * 4 + zt], dev)))

    def spread(buf, ss, rs):
        def far(kx):
            return rcopy(buf.at[0], buf.at[kx], ss.at[kx], rs.at[kx], dense_dev(kx, 0)[0])

        def near(kx):
            return rcopy(buf.at[kx], buf.at[4 + kx], ss.at[4 + kx], rs.at[4 + kx], dense_dev(0, 1)[0])

        for kx in (2, 1, 3):
            far(kx).start()
        near(0).start()

        def relay():
            for kx in (1, 3, 2):
                far(kx).wait_recv()
                near(kx).start()

        def finish():
            for kx in range(4):
                near(kx).wait_recv()

        def drain():
            for kx in range(4):
                near(kx).wait_send()
            for kx in (1, 2, 3):
                far(kx).wait_send()

        return relay, finish, drain

    ld_pool.wait()
    ld_v.wait()
    hid_g[0] = lax.dot_general(pool_v[...], v_v[...], NT, preferred_element_type=F32).astype(BF16)
    hid_relay, hid_finish, hid_drain = spread(hid_g, hg_s, hg_r)
    ld_u.wait()

    part = jnp.zeros((B, 128), F32)
    for j in range(8):
        cols = pl.ds(j * 512, 512)
        sc = jnp.dot(hid_g[0], u_v[:, cols], preferred_element_type=F32) + bias[:, cols]
        scale_v[:, cols] = sc
        f = pool_v[:, cols].astype(F32)
        prod = (f * sc + f) * head[:, cols]
        part = part + (prod[:, 0:128] + prod[:, 128:256]) + (prod[:, 256:384] + prod[:, 384:512])
    logits = jnp.sum(part, axis=1, keepdims=True)
    chance = 1.0 / (1.0 + jnp.exp(-jnp.broadcast_to(logits, (B, 128))))
    lgb = fnw_c * (chance - lab_c)
    lg_row = jnp.concatenate([lgb, jnp.zeros((96, 128), F32)], axis=0).T[:8]
    lg_g[0] = lg_row
    lgc = [go(rcopy(lg_g.at[0], lg_g.at[kc * 4 + kx], lg_s.at[k], lg_r.at[k], dense_dev(kx, kc)[0]))
           for k, (kx, kc) in enumerate(DENSE)]
    lgw = jnp.concatenate([lgb, lgb], axis=1)

    low = jnp.zeros((B, R), F32)
    for j in range(16):
        cols = pl.ds(j * W, W)
        f = pool_v[:, cols].astype(F32)
        sg = (lgw * head[:, cols]) * f
        low = low + lax.dot_general(sg.astype(BF16), u_v[:, cols], NT, preferred_element_type=F32)
        mixed = f * scale_v[:, cols] + f
        sums = jnp.concatenate(
            [jnp.sum(sg, axis=0, keepdims=True), jnp.sum(lgw * mixed, axis=0, keepdims=True),
             jnp.zeros((6, W), F32)], axis=0)
        for b in range(2):
            m = (((j // 2) % 2) * 2 + b) * 2 + j % 2
            small_s[m, :, pl.ds((j // 4) * E, E)] = sums[:, b * E:(b + 1) * E]
    low_g[0] = low.astype(BF16)
    low_relay, low_finish, low_drain = spread(low_g, lo_s, lo_r)

    def z_copy(f, k, dev):
        return rcopy(ig_s.at[f, k], e1.at[f, me], z_s.at[f, k], z_r.at[f, k], dev)

    for k, off in enumerate(GROUP + [(0, 0)]):
        dev, m = group_dev(*off)
        for b in range(2):
            cols = pl.ds(pl.multiple_of(((m // 2) * 4 + b * 2 + m % 2) * W, W), W)
            ig = ((lgw * head[:, cols]) * (scale_v[:, cols] + 1.0) + jnp.dot(
                low_g[0], v_v[:, cols], preferred_element_type=F32)).astype(BF16)
            for f in range(2):
                if k < 7:
                    ig_s[f, k, b] = ig[:, f * E:(f + 1) * E]
                else:
                    e1[f, me, b] = ig[:, f * E:(f + 1) * E]
        if k < 7:
            go(z_copy(0, k, dev))
    for k, off in enumerate(GROUP):
        go(z_copy(1, k, group_dev(*off)[0]))
    smc = []
    for k, (kx, kc) in enumerate(DENSE):
        dev, m = dense_dev(kx, kc)
        smc.append(go(rcopy(small_s.at[m], small_g.at[k], sm_s.at[k], sm_r.at[k], dev)))

    def y1_copy(f, m):
        return rcopy(e1.at[f, m, yh], gath.at[f, 1, m], y1_s.at[f, m], y1_r.at[f, m], y_dev(0, 1))

    def y3_copy(f, m):
        return rcopy(e1.at[f, m, 1 - yh], gath.at[f, 3, m], y3_s.at[f, m], y3_r.at[f, m], y_dev(1, 1))

    def y2_copy(f, m):
        return rcopy(gath.at[f, 3, m], gath.at[f, 2, m], y2_s.at[f, m], y2_r.at[f, m], y_dev(0, 1))

    def forward(f, m):
        y3_copy(f, m).start()
        y1_copy(f, m).start()
        gath[f, 0, m] = e1[f, m, yh]

    def forward_all(f, order):
        for kz, kc in order:
            z_copy(f, GROUP.index((kz, kc)), (h, l)).wait_recv()
            forward(f, src_of(kz, kc))

    def relay_all(f):
        for kz, kc in [(0, 0)] + ARRIVE:
            m = src_of(kz, kc)
            y3_copy(f, m).wait_recv()
            y2_copy(f, m).start()

    forward(0, me)
    forward_all(0, ARRIVE[:1])
    forward(1, me)

    ld_ids.wait()
    ld_lens.wait()
    lane = lax.broadcasted_iota(jnp.int32, (8, 640), 1)
    for ys in range(4):
        for g in range(2):
            out = jnp.zeros((8, 640), jnp.int32)
            for i in range(4):
                hs = (2 * g + i // 2) * 4 + (ys // 2) * 2 + i % 2
                win = pl.ds(hs * 1280 + (ys % 2) * 640, 640)
                ln = lens[:, win]
                got = jnp.concatenate([jnp.where(ln > s, ids[s, :, win], -1) for s in range(4)], axis=0)
                got = pltpu.roll(got, (160 * i + 640 - 160 * x) % 640, 1)
                out = jnp.where((lane >= 160 * i) & (lane < 160 * (i + 1)), got, out)
            target[:, pl.ds((ys * 2 + g) * 640, 640)] = out.astype(F32)
    for f in range(2):
        t = [target[pl.ds(s * 2 + f, 1), :] for s in range(4)]
        e01, e02, e03 = t[0] == t[1], t[0] == t[2], t[0] == t[3]
        e12, e13, e23 = t[1] == t[2], t[1] == t[3], t[2] == t[3]
        one = lambda m: jnp.where(m, 1.0, 0.0)
        weight[pl.ds(f, 1), :] = 1.0 + one(e01) + one(e02) + one(e03)
        weight[pl.ds(2 + f, 1), :] = 1.0 + one(e12) + one(e13)
        weight[pl.ds(4 + f, 1), :] = 1.0 + one(e23)
        weight[pl.ds(6 + f, 1), :] = jnp.ones_like(t[0])
        target[pl.ds(2 + f, 1), :] = jnp.where(e01, -1.0, t[1])
        target[pl.ds(4 + f, 1), :] = jnp.where(e02 | e12, -1.0, t[2])
        target[pl.ds(6 + f, 1), :] = jnp.where(e03 | e13 | e23, -1.0, t[3])

    forward_all(0, ARRIVE[1:])
    acc[...] = jnp.zeros_like(acc)

    def d1_copies(k):
        kz = (2, 1, 3)[k]
        dev, zz = group_dev(kz, 0)[0], (z + kz) % 4
        return (rcopy(dense_s.at[zz], dense_r.at[k], dn_s.at[k], dn_r.at[k], dev),
                rcopy(tsmall_s.at[zz], tsmall_r.at[k], ts_s.at[k], ts_r.at[k], dev))

    def dense_products():
        mine = x * 2 + c
        own_cols = [dense_cols(mine, zt) for zt in range(4)]
        for zt in range(4):
            pool_g[0, :, pl.ds(zt * E, E)] = pool_v[:, own_cols[zt]]
        own_head = jnp.concatenate([head[:, own_cols[zt]] for zt in range(4)], axis=1)

        for cp in pg + lgc:
            cp.wait_recv()
        hid_finish()
        for k in range(8):
            lgk = jnp.concatenate([lg_g[k]] * 16, axis=0).T[:B]
            lgk = jnp.concatenate([lgk] * 4, axis=1)
            half_g[pl.ds(k * B, B), :] = ((lgk * own_head) * pool_g[k].astype(F32)).astype(BF16)
        dense_s[:, :, :, pl.ds(0, R)] = lax.dot_general(
            half_g[...], hid_g[...].reshape(KC, R), TN, preferred_element_type=F32
        ).astype(BF16).reshape(4, 4, 32, R)
        low_finish()
        ld_table.wait()
        for cp in smc:
            cp.wait_recv()
        dense_s[:, :, :, pl.ds(R, R)] = lax.dot_general(
            pool_g[...].reshape(KC, R), low_g[...].reshape(KC, R), TN, preferred_element_type=F32
        ).astype(BF16).reshape(4, 4, 32, R)
        tot = small_s[mine]
        for k in range(7):
            tot = tot + small_g[k]
        tsmall_s[...] = jnp.concatenate([tot, jnp.zeros((120, R), F32)], axis=0).T.reshape(4, 4, 32, 128)
        for k in range(3):
            for cp in d1_copies(k):
                cp.start()

    iota = lax.broadcasted_iota(jnp.int32, (16, KC), 0).astype(F32).astype(BF16)

    def x_off(kx):
        return (2 - kx + (kx // 2) * 3 + (kx // 3) * 2) % 4

    def x_copy(f, kx):
        return rcopy(x_s.at[f, kx], x_r.at[f, kx], xs_s.at[f, kx], xs_r.at[f, kx], x_dev(x_off(kx)))

    def d2_copy(k):
        xx = (x + k + 1) % 4
        return rcopy(d2_s.at[xx], d2_r.at[x], d2_ss.at[k], d2_rs.at[k], x_dev(k + 1))

    def d3_copy(k):
        ka, kb = YS[k]
        yy = ((yh + ka) % 2) * 2 + (yl + kb) % 2
        return rcopy(d2_r.at[yy], d3_r.at[k], d3_ss.at[k], d3_rs.at[k], y_dev(ka, kb))

    def update(f):
        for kx in range(3):
            x_copy(f, kx).wait_recv()
        g = acc[3, :, pl.ds(f * E, E)] + (x_r[f, 0].astype(F32) + x_r[f, 1].astype(F32)) + x_r[f, 2].astype(F32)
        new = column(accum[pl.ds(f, 1), :]) + jnp.sum(g * g, axis=1, keepdims=True) * (1.0 / E)
        rows = pl.ds(f, RC, stride=2)
        out_rows[rows, :] = table[rows, :] - learn_rate * g / (jnp.sqrt(new) + epsilon)
        out_accum[pl.ds(f, 1), :] = new.T[:1]

    def step(s, carry):
        f, dd = s // 4, s % 4
        d = dd + (dd // 2) * (1 - 2 * (dd % 2))

        @pl.when(s == 1)
        def _():
            relay_all(0)
            forward_all(1, ARRIVE)

        @pl.when(s == 2)
        def _():
            hid_relay()

        @pl.when(s == 3)
        def _():
            low_relay()
            relay_all(1)

        @pl.when(s == 4)
        def _():
            dense_products()

        @pl.when(s == 6)
        def _():
            for k in range(3):
                for cp in d1_copies(k):
                    cp.wait_recv()
            d2_s[:, :, pl.ds(0, 2 * R)] = (
                (dense_s[z].astype(F32) + dense_r[0].astype(F32))
                + (dense_r[1].astype(F32) + dense_r[2].astype(F32)))
            d2_s[:, :, pl.ds(2 * R, 128)] = (tsmall_s[z] + tsmall_r[0]) + (tsmall_r[1] + tsmall_r[2])
            d2_r[x] = d2_s[x]
            for k in range(3):
                d2_copy(k).start()

        @pl.when(s == 7)
        def _():
            for k in range(3):
                d2_copy(k).wait_recv()
            for k in range(3):
                d3_copy(k).start()
            update(0)

        @pl.when(dd == 1)
        def _():
            def one(m, cc):
                y1_copy(f, m).wait_recv()
                return cc
            lax.fori_loop(0, 8, one, 0)

        @pl.when(dd == 3)
        def _():
            def one(m, cc):
                y2_copy(f, m).wait_recv()
                return cc
            lax.fori_loop(0, 8, one, 0)

        src = ((yh + d // 2) % 2) * 2 + (yl + d % 2) % 2
        lanes = pl.ds(pl.multiple_of(src * KC, 128), KC)
        fcols = pl.ds(pl.multiple_of(f * E, E), E)

        def chunk_step(kx, cc):
            base = (yl * 4 + (x + x_off(kx)) % 4) * RC
            tt = [target[pl.ds(q * 2 + f, 1), lanes] for q in range(4)]
            ws = [jnp.broadcast_to(weight[pl.ds(q * 2 + f, 1), lanes], (16, KC)).astype(BF16)
                  for q in range(4)]
            tiles = []
            for sb in range(RC // 256):
                low_row = (base + sb * 256).astype(F32)
                ts = [jnp.broadcast_to(tt[q] - low_row, (16, KC)).astype(BF16) for q in range(4)]
                for i in range(16):
                    it = iota + jnp.asarray(16 * i, BF16)
                    cnt = jnp.zeros((16, KC), BF16)
                    for q in range(4):
                        cnt = jnp.where(it == ts[q], ws[q], cnt)
                    tiles.append(cnt)
            counts = jnp.concatenate(tiles, axis=0)
            g = gath[f, d].reshape(KC, E)
            acc[kx, :, fcols] += jnp.dot(counts, g, preferred_element_type=F32)

            @pl.when((dd == 3) & (kx < 3))
            def _():
                x_s[f, kx] = acc[kx, :, fcols].astype(BF16)
                x_copy(f, kx).start()
            return cc

        return lax.fori_loop(0, 4, chunk_step, carry)

    lax.fori_loop(0, 8, step, 0)

    for k in range(3):
        d3_copy(k).wait_recv()
    tot = (d2_r[yh * 2 + yl] + d3_r[0]) + (d3_r[1] + d3_r[2])
    out_u[...] = tot[:, :R]
    out_v[...] = tot[:, R:2 * R]
    out_small[...] = tot[:, 2 * R:]
    update(1)

    for f in range(2):
        for kx in range(3):
            x_copy(f, kx).wait_send()

        def drain(m, cc):
            y1_copy(f, m).wait_send()
            y3_copy(f, m).wait_send()
            y2_copy(f, m).wait_send()
            return cc
        lax.fori_loop(0, 8, drain, 0)
    for k in range(3):
        d2_copy(k).wait_send()
        d3_copy(k).wait_send()
        for cp in d1_copies(k):
            cp.wait_send()
    hid_drain()
    low_drain()
    for cp in sends:
        cp.wait_send()


def fused(*operands):
    any_, vmem = pl.BlockSpec(memory_space=pl.ANY), pl.BlockSpec(memory_space=pltpu.VMEM)
    V, S = pltpu.VMEM, lambda *n: pltpu.SemaphoreType.DMA(n)
    return pl.pallas_call(
        kernel,
        out_shape=(
            jax.ShapeDtypeStruct((32, R), F32),
            jax.ShapeDtypeStruct((32, R), F32),
            jax.ShapeDtypeStruct((32, 128), F32),
            jax.ShapeDtypeStruct((2 * RC, E), F32),
            jax.ShapeDtypeStruct((2, RC), F32),
        ),
        in_specs=[any_, any_, any_, vmem, vmem, vmem, vmem, any_, any_, any_, vmem],
        out_specs=(vmem,) * 5,
        scratch_shapes=[
            V((B, D), BF16), V((R, D), BF16), V((R, D), BF16), V((B, D), F32),
            V((4, 2, 20480), jnp.int32), V((2, 20480), jnp.int32), V((2 * RC, E), F32),
            V((8, 4 * KC), F32), V((8, 4 * KC), F32), V((8, 256), F32),
            V((G, B, R), BF16), V((G, B, R), BF16), V((G, B, R), BF16), V((G, 8, 256), F32),
            V((G, 8, R), F32), V((G - 1, 8, R), F32),
            V((2, G - 1, 2, B, E), BF16), V((2, G, 2, B, E), BF16), V((2, 4, G, B, E), BF16), V((KC, R), BF16),
            V((4, 4, 32, 2 * R), BF16), V((3, 4, 32, 2 * R), BF16),
            V((4, 4, 32, 128), F32), V((3, 4, 32, 128), F32),
            V((4, 32, 2 * R + 128), F32), V((4, 32, 2 * R + 128), F32), V((3, 32, 2 * R + 128), F32),
            V((4, RC, W), F32), V((2, 3, RC, E), BF16), V((2, 3, RC, E), BF16),
            S(6), S(28), S(28), S(8), S(8), S(8), S(8), S(7), S(7), S(7), S(7),
            S(2, 7), S(2, 7), S(2, 8), S(2, 8), S(2, 8), S(2, 8), S(2, 8), S(2, 8),
            S(3), S(3), S(3), S(3), S(3), S(3), S(3), S(3), S(2, 3), S(2, 3),
        ],
        compiler_params=pltpu.CompilerParams(
            collective_id=0, has_side_effects=True, vmem_limit_bytes=60 * 2**20
        ),
        cost_estimate=pl.CostEstimate(flops=16 * 10**9, bytes_accessed=12 * 10**6, transcendentals=160),
    )(*operands)


def body(
    pooled, cross_v, cross_u, cross_bias, head_weight, labels, fn_weight,
    row_ids, bag_lengths, table_rows, row_accum,
):
    grad_u, grad_v, small, rows, accum = fused(
        pooled, cross_v, cross_u, cross_bias[None], head_weight[None], labels[None], fn_weight[None],
        row_ids, bag_lengths, table_rows.reshape(2 * RC, E), row_accum.T,
    )
    return grad_u.T, grad_v.T, small[:, :2].T, rows.reshape(RC, 2, E), accum.T


def solution(mesh):
    placed = (
        P(("hst", "local"), None), P(), P(), P(), P(), P(("hst", "local")), P(("hst", "local")),
        P(None, "hst", None), P("hst", None), P("local", "hst", None), P("local", "hst"),
    )
    both = P(None, ("hst", "local"))
    return jax.shard_map(
        body, mesh=mesh, in_specs=placed,
        out_specs=(both, both, both, P("local", "hst", None), P("local", "hst")),
        check_vma=False,
    )
```

```python
import jax
import jax.numpy as jnp
from jax import lax
from jax.experimental import pallas as pl
from jax.experimental.pallas import tpu as pltpu
from jax.sharding import PartitionSpec as P

learn_rate = 0.05
epsilon = 1e-08
MESH = pl.DeviceIdType.MESH
F32 = jnp.float32
BF16 = jnp.bfloat16

B = 160
R = 512
D = 4096
W = 256
E = 128
G = 8
KC = G * B
RC = 1024
NT = (((1,), (1,)), ((), ()))
TN = (((0,), (0,)), ((), ()))

GROUP = [(2, 0), (2, 1), (1, 0), (3, 0), (1, 1), (3, 1), (0, 1)]
ARRIVE = [(0, 1), (1, 0), (3, 0), (1, 1), (3, 1), (2, 0), (2, 1)]
NEAR = [(0, 0)]
YS = [(0, 1), (1, 0), (1, 1)]
DENSE = [(2, 0), (2, 1), (1, 0), (3, 0), (1, 1), (3, 1), (0, 1)]


def kernel(
    pooled, v_hbm, u_hbm, bias, head, labels, fn_weight, ids_hbm, lens_hbm,
    out_dense, out_rows,
    pool_v, v_v, u_v, scale_v, ids, lens, target, weight, cols_v,
    pool_g, hid_g, low_g, lg_g, small_s, small_g,
    ig_s, e1, gath, half_g,
    dense_s, dense_r, tsmall_s, tsmall_r, d2_s, d2_r, d3_r,
    acc, x_s, x_r,
    loc_sem, pg_s, pg_r, hg_s, hg_r, lo_s, lo_r, lg_s, lg_r, sm_s, sm_r,
    z_s, z_r, y1_s, y1_r, y3_s, y3_r, y2_s, y2_r, dn_s, dn_r, ts_s, ts_r, d2_ss, d2_rs, d3_ss, d3_rs, xs_s, xs_r,
):
    h = lax.axis_index("hst")
    l = lax.axis_index("local")
    z, yh, c = h // 4, (h // 2) % 2, h % 2
    yl, x = l // 4, l % 4
    me = z * 2 + c

    def group_dev(kz, kc):
        zz, cc = (z + kz) % 4, (c + kc) % 2
        return (zz * 4 + yh * 2 + cc, l), zz * 2 + cc

    def y_dev(ka, kb):
        return (z * 4 + ((yh + ka) % 2) * 2 + c, ((yl + kb) % 2) * 4 + x)

    def x_dev(kx):
        return (h, yl * 4 + (x + kx) % 4)

    def dense_dev(kx, kc):
        xx, cc = (x + kx) % 4, (c + kc) % 2
        return (z * 4 + yh * 2 + cc, yl * 4 + xx), xx * 2 + cc

    def dense_cols(m, zt):
        col = (zt * 4 + (m // 4) * 2 + m % 2) * W + ((m // 2) % 2) * E
        return pl.ds(pl.multiple_of(col, E), E)

    def rcopy(src, dst, ss, rs, dev):
        return pltpu.make_async_remote_copy(
            src_ref=src, dst_ref=dst, send_sem=ss, recv_sem=rs, device_id=dev, device_id_type=MESH
        )

    def src_of(kz, kc):
        return ((z - kz + 4) % 4) * 2 + (c + kc) % 2

    barrier = pltpu.get_barrier_semaphore()
    partners = [group_dev(*o)[0] for o in GROUP] + [y_dev(*o) for o in YS] + [dense_dev(*o)[0] for o in DENSE[:-1]]
    for dev in partners:
        pl.semaphore_signal(barrier, inc=1, device_id=dev, device_id_type=MESH)

    def load(src, dst, i):
        cp = pltpu.make_async_copy(src, dst, loc_sem.at[i])
        cp.start()
        return cp

    ld_pool, ld_v, ld_u = load(pooled, pool_v, 2), load(v_hbm, v_v, 3), load(u_hbm, u_v, 4)

    cols_v[...] = jnp.zeros_like(cols_v)
    cols_v[pl.ds(0, 1), pl.ds(0, B)] = labels[...].astype(F32)
    cols_v[pl.ds(1, 1), pl.ds(0, B)] = fn_weight[...].astype(F32)

    def column(row):
        return jnp.broadcast_to(row, (128, row.shape[1])).T

    lab_c = column(cols_v[pl.ds(0, 1), :])[:B]
    fnw_c = column(cols_v[pl.ds(1, 1), :])[:B]

    pl.semaphore_wait(barrier, len(partners))

    sends = []

    def go(copy):
        copy.start()
        sends.append(copy)
        return copy

    pg = []
    for k, (kx, kc) in enumerate(DENSE):
        dev, m = dense_dev(kx, kc)
        for zt in range(4):
            pg.append(go(rcopy(pooled.at[:, dense_cols(m, zt)], pool_g.at[kc * 4 + kx, :, pl.ds(zt * E, E)],
                               pg_s.at[k * 4 + zt], pg_r.at[k * 4 + zt], dev)))

    def spread(buf, ss, rs):
        def far(kx):
            return rcopy(buf.at[0], buf.at[kx], ss.at[kx], rs.at[kx], dense_dev(kx, 0)[0])

        def near(kx):
            return rcopy(buf.at[kx], buf.at[4 + kx], ss.at[4 + kx], rs.at[4 + kx], dense_dev(0, 1)[0])

        for kx in (2, 1, 3):
            far(kx).start()
        near(0).start()

        def relay():
            for kx in (1, 3, 2):
                far(kx).wait_recv()
                near(kx).start()

        def finish():
            for kx in range(4):
                near(kx).wait_recv()

        def drain():
            for kx in range(4):
                near(kx).wait_send()
            for kx in (1, 2, 3):
                far(kx).wait_send()

        return relay, finish, drain

    ld_ids, ld_lens = load(ids_hbm, ids, 0), load(lens_hbm, lens, 1)

    ld_pool.wait()
    ld_v.wait()
    hid_g[0] = lax.dot_general(pool_v[...], v_v[...], NT, preferred_element_type=F32).astype(BF16)
    hid_relay, hid_finish, hid_drain = spread(hid_g, hg_s, hg_r)
    ld_u.wait()

    part = jnp.zeros((B, 128), F32)
    for j in range(8):
        cols = pl.ds(j * 512, 512)
        sc = jnp.dot(hid_g[0], u_v[:, cols], preferred_element_type=F32) + bias[:, cols]
        scale_v[:, cols] = sc
        f = pool_v[:, cols].astype(F32)
        prod = (f * sc + f) * head[:, cols]
        part = part + (prod[:, 0:128] + prod[:, 128:256]) + (prod[:, 256:384] + prod[:, 384:512])
    logits = jnp.sum(part, axis=1, keepdims=True)
    chance = 1.0 / (1.0 + jnp.exp(-jnp.broadcast_to(logits, (B, 128))))
    lgb = fnw_c * (chance - lab_c)
    lg_row = jnp.concatenate([lgb, jnp.zeros((96, 128), F32)], axis=0).T[:8]
    lg_g[0] = lg_row
    lgc = [go(rcopy(lg_g.at[0], lg_g.at[kc * 4 + kx], lg_s.at[k], lg_r.at[k], dense_dev(kx, kc)[0]))
           for k, (kx, kc) in enumerate(DENSE)]
    lgw = jnp.concatenate([lgb, lgb], axis=1)

    low = jnp.zeros((B, R), F32)
    for j in range(16):
        cols = pl.ds(j * W, W)
        f = pool_v[:, cols].astype(F32)
        sg = (lgw * head[:, cols]) * f
        low = low + lax.dot_general(sg.astype(BF16), u_v[:, cols], NT, preferred_element_type=F32)
        mixed = f * scale_v[:, cols] + f
        sums = jnp.concatenate(
            [jnp.sum(sg, axis=0, keepdims=True), jnp.sum(lgw * mixed, axis=0, keepdims=True),
             jnp.zeros((6, W), F32)], axis=0)
        for b in range(2):
            m = (((j // 2) % 2) * 2 + b) * 2 + j % 2
            small_s[m, :, pl.ds((j // 4) * E, E)] = sums[:, b * E:(b + 1) * E]
    low_g[0] = low.astype(BF16)
    low_relay, low_finish, low_drain = spread(low_g, lo_s, lo_r)

    def z_copy(f, k, dev):
        return rcopy(ig_s.at[f, k], e1.at[f, me], z_s.at[f, k], z_r.at[f, k], dev)

    for k, off in enumerate(GROUP + [(0, 0)]):
        dev, m = group_dev(*off)
        for b in range(2):
            cols = pl.ds(pl.multiple_of(((m // 2) * 4 + b * 2 + m % 2) * W, W), W)
            ig = ((lgw * head[:, cols]) * (scale_v[:, cols] + 1.0) + jnp.dot(
                low_g[0], v_v[:, cols], preferred_element_type=F32)).astype(BF16)
            for f in range(2):
                if k < 7:
                    ig_s[f, k, b] = ig[:, f * E:(f + 1) * E]
                else:
                    e1[f, me, b] = ig[:, f * E:(f + 1) * E]
        if k < 7:
            go(z_copy(0, k, dev))
    smc = []
    for k, (kx, kc) in enumerate(DENSE):
        dev, m = dense_dev(kx, kc)
        smc.append(go(rcopy(small_s.at[m], small_g.at[k], sm_s.at[k], sm_r.at[k], dev)))

    def y1_copy(f, m):
        return rcopy(e1.at[f, m, yh], gath.at[f, 1, m], y1_s.at[f, m], y1_r.at[f, m], y_dev(0, 1))

    def y3_copy(f, m):
        return rcopy(e1.at[f, m, 1 - yh], gath.at[f, 3, m], y3_s.at[f, m], y3_r.at[f, m], y_dev(1, 1))

    def y2_copy(f, m):
        return rcopy(gath.at[f, 3, m], gath.at[f, 2, m], y2_s.at[f, m], y2_r.at[f, m], y_dev(0, 1))

    def forward(f, m):
        y3_copy(f, m).start()
        y1_copy(f, m).start()
        gath[f, 0, m] = e1[f, m, yh]

    def forward_all(f, order):
        for kz, kc in order:
            z_copy(f, GROUP.index((kz, kc)), (h, l)).wait_recv()
            forward(f, src_of(kz, kc))

    def relay_all(f, order):
        for kz, kc in order:
            m = src_of(kz, kc)
            y3_copy(f, m).wait_recv()
            y2_copy(f, m).start()

    forward(0, me)
    forward_all(0, ARRIVE[:1])
    forward(1, me)

    ld_ids.wait()
    ld_lens.wait()
    lane = lax.broadcasted_iota(jnp.int32, (8, 640), 1)
    for ys in range(4):
        for g in range(2):
            out = jnp.zeros((8, 640), jnp.int32)
            for i in range(4):
                hs = (2 * g + i // 2) * 4 + (ys // 2) * 2 + i % 2
                win = pl.ds(hs * 1280 + (ys % 2) * 640, 640)
                ln = lens[:, win]
                got = jnp.concatenate([jnp.where(ln > s, ids[s, :, win], -1) for s in range(4)], axis=0)
                got = pltpu.roll(got, (160 * i + 640 - 160 * x) % 640, 1)
                out = jnp.where((lane >= 160 * i) & (lane < 160 * (i + 1)), got, out)
            target[:, pl.ds((ys * 2 + g) * 640, 640)] = out.astype(F32)
    for f in range(2):
        t = [target[pl.ds(s * 2 + f, 1), :] for s in range(4)]
        e01, e02, e03 = t[0] == t[1], t[0] == t[2], t[0] == t[3]
        e12, e13, e23 = t[1] == t[2], t[1] == t[3], t[2] == t[3]
        one = lambda m: jnp.where(m, 1.0, 0.0)
        weight[pl.ds(f, 1), :] = 1.0 + one(e01) + one(e02) + one(e03)
        weight[pl.ds(2 + f, 1), :] = 1.0 + one(e12) + one(e13)
        weight[pl.ds(4 + f, 1), :] = 1.0 + one(e23)
        weight[pl.ds(6 + f, 1), :] = jnp.ones_like(t[0])
        target[pl.ds(2 + f, 1), :] = jnp.where(e01, -1.0, t[1])
        target[pl.ds(4 + f, 1), :] = jnp.where(e02 | e12, -1.0, t[2])
        target[pl.ds(6 + f, 1), :] = jnp.where(e03 | e13 | e23, -1.0, t[3])

    forward_all(0, ARRIVE[1:])
    for k, off in enumerate(GROUP):
        go(z_copy(1, k, group_dev(*off)[0]))
    acc[...] = jnp.zeros_like(acc)

    def d1_copies(k):
        kz = (2, 1, 3)[k]
        dev, zz = group_dev(kz, 0)[0], (z + kz) % 4
        return (rcopy(dense_s.at[zz], dense_r.at[k], dn_s.at[k], dn_r.at[k], dev),
                rcopy(tsmall_s.at[zz], tsmall_r.at[k], ts_s.at[k], ts_r.at[k], dev))

    def dense_products():
        mine = x * 2 + c
        own_cols = [dense_cols(mine, zt) for zt in range(4)]
        for zt in range(4):
            pool_g[0, :, pl.ds(zt * E, E)] = pool_v[:, own_cols[zt]]
        own_head = jnp.concatenate([head[:, own_cols[zt]] for zt in range(4)], axis=1)

        for cp in pg + lgc:
            cp.wait_recv()
        hid_finish()
        for k in range(8):
            lgk = jnp.concatenate([lg_g[k]] * 16, axis=0).T[:B]
            lgk = jnp.concatenate([lgk] * 4, axis=1)
            half_g[pl.ds(k * B, B), :] = ((lgk * own_head) * pool_g[k].astype(F32)).astype(BF16)
        dense_s[:, :, :, pl.ds(0, R)] = lax.dot_general(
            half_g[...], hid_g[...].reshape(KC, R), TN, preferred_element_type=F32
        ).astype(BF16).reshape(4, 4, 32, R)
        low_finish()
        for cp in smc:
            cp.wait_recv()
        dense_s[:, :, :, pl.ds(R, R)] = lax.dot_general(
            pool_g[...].reshape(KC, R), low_g[...].reshape(KC, R), TN, preferred_element_type=F32
        ).astype(BF16).reshape(4, 4, 32, R)
        tot = small_s[mine]
        for k in range(7):
            tot = tot + small_g[k]
        for zt in range(4):
            tsmall_s[zt] = tot[:, zt * E:(zt + 1) * E]
        for k in range(3):
            for cp in d1_copies(k):
                cp.start()

    iota = lax.broadcasted_iota(jnp.int32, (16, KC), 0).astype(F32).astype(BF16)

    def x_off(kx):
        return (2 - kx + (kx // 2) * 3 + (kx // 3) * 2) % 4

    def x_copy(f, kx):
        return rcopy(x_s.at[f, kx], x_r.at[f, kx], xs_s.at[f, kx], xs_r.at[f, kx], x_dev(x_off(kx)))

    def d2_copy(k):
        xx = (x + k + 1) % 4
        return rcopy(d2_s.at[xx], d2_r.at[x], d2_ss.at[k], d2_rs.at[k], x_dev(k + 1))

    def d3_copy(k):
        ka, kb = YS[k]
        yy = ((yh + ka) % 2) * 2 + (yl + kb) % 2
        return rcopy(d2_r.at[yy], d3_r.at[k], d3_ss.at[k], d3_rs.at[k], y_dev(ka, kb))

    def row_sums(f):
        for kx in range(3):
            x_copy(f, kx).wait_recv()
        out_rows[:, pl.ds(f * E, E)] = (
            acc[3, :, pl.ds(f * E, E)] + (x_r[f, 0].astype(F32) + x_r[f, 1].astype(F32)) + x_r[f, 2].astype(F32))

    def wait_y(copy, f):
        def one(m, cc):
            copy(f, m).wait_recv()
            return cc
        lax.fori_loop(0, 8, one, 0)

    def sum_along_z():
        for k in range(3):
            for cp in d1_copies(k):
                cp.wait_recv()
        d2_s[:, :, pl.ds(0, 2 * R)] = (
            (dense_s[z].astype(F32) + dense_r[0].astype(F32))
            + (dense_r[1].astype(F32) + dense_r[2].astype(F32)))
        few = (tsmall_s[z] + tsmall_r[0]) + (tsmall_r[1] + tsmall_r[2])
        d2_s[:, :, pl.ds(2 * R, 128)] = jnp.concatenate(
            [few, jnp.zeros((120, 128), F32)], axis=0).T.reshape(4, 32, 128)
        d2_r[x] = d2_s[x]
        for k in range(3):
            d2_copy(k).start()

    def blocks_along_y():
        for k in range(3):
            d2_copy(k).wait_recv()
        for k in range(3):
            d3_copy(k).start()

    def at(t, when, act):
        pl.when(t == when)(act)

    def step(t, carry):
        late = t // 24
        s = (1 - late) * (t // 4) + late * (6 + t % 2)
        kx = (1 - late) * (t % 4) + late * ((t - 24) // 2)
        f, dd = s // 4, s % 4
        d = dd + (dd // 2) * (1 - 2 * (dd % 2))
        at(t, 1, lambda: relay_all(0, NEAR + ARRIVE))
        at(t, 4, lambda: wait_y(y1_copy, 0))
        at(t, 7, lambda: forward_all(1, ARRIVE))
        at(t, 10, hid_relay)
        at(t, 11, lambda: relay_all(1, NEAR + ARRIVE[:3]))
        at(t, 12, lambda: wait_y(y2_copy, 0))
        at(t, 12, low_relay)
        at(t, 13, dense_products)
        at(t, 15, lambda: relay_all(1, ARRIVE[3:]))
        at(t, 20, lambda: wait_y(y1_copy, 1))
        at(t, 24, sum_along_z)
        at(t, 24, lambda: wait_y(y2_copy, 1))
        at(t, 30, blocks_along_y)
        at(t, 30, lambda: row_sums(0))

        src = ((yh + d // 2) % 2) * 2 + (yl + d % 2) % 2
        lanes = pl.ds(pl.multiple_of(src * KC, 128), KC)
        fcols = pl.ds(pl.multiple_of(f * E, E), E)

        base = (yl * 4 + (x + x_off(kx)) % 4) * RC
        tt = [target[pl.ds(q * 2 + f, 1), lanes] for q in range(4)]
        ws = [jnp.broadcast_to(weight[pl.ds(q * 2 + f, 1), lanes], (16, KC)).astype(BF16)
              for q in range(4)]
        tiles = []
        for sb in range(RC // 256):
            low_row = (base + sb * 256).astype(F32)
            ts = [jnp.broadcast_to(tt[q] - low_row, (16, KC)).astype(BF16) for q in range(4)]
            for i in range(16):
                it = iota + jnp.asarray(16 * i, BF16)
                cnt = jnp.zeros((16, KC), BF16)
                for q in range(4):
                    cnt = jnp.where(it == ts[q], ws[q], cnt)
                tiles.append(cnt)
        counts = jnp.concatenate(tiles, axis=0)
        g = gath[f, d].reshape(KC, E)
        acc[kx, :, fcols] += jnp.dot(counts, g, preferred_element_type=F32)

        @pl.when((dd == 3) & (kx < 3))
        def _():
            x_s[f, kx] = acc[kx, :, fcols].astype(BF16)
            x_copy(f, kx).start()
        return carry

    lax.fori_loop(0, 32, step, 0)

    for k in range(3):
        d3_copy(k).wait_recv()
    out_dense[...] = (d2_r[yh * 2 + yl] + d3_r[0]) + (d3_r[1] + d3_r[2])
    row_sums(1)

    for f in range(2):
        for kx in range(3):
            x_copy(f, kx).wait_send()

        def drain(m, cc):
            y1_copy(f, m).wait_send()
            y3_copy(f, m).wait_send()
            y2_copy(f, m).wait_send()
            return cc
        lax.fori_loop(0, 8, drain, 0)
    for k in range(3):
        d2_copy(k).wait_send()
        d3_copy(k).wait_send()
        for cp in d1_copies(k):
            cp.wait_send()
    hid_drain()
    low_drain()
    for cp in sends:
        cp.wait_send()


def fused(*operands):
    any_, vmem = pl.BlockSpec(memory_space=pl.ANY), pl.BlockSpec(memory_space=pltpu.VMEM)
    V, S = pltpu.VMEM, lambda *n: pltpu.SemaphoreType.DMA(n)
    return pl.pallas_call(
        kernel,
        out_shape=(jax.ShapeDtypeStruct((32, 2 * R + 128), F32), jax.ShapeDtypeStruct((RC, W), F32)),
        in_specs=[any_, any_, any_, vmem, vmem, vmem, vmem, any_, any_],
        out_specs=(vmem, vmem),
        scratch_shapes=[
            V((B, D), BF16), V((R, D), BF16), V((R, D), BF16), V((B, D), F32),
            V((4, 2, 20480), jnp.int32), V((2, 20480), jnp.int32),
            V((8, 4 * KC), F32), V((8, 4 * KC), F32), V((8, 256), F32),
            V((G, B, R), BF16), V((G, B, R), BF16), V((G, B, R), BF16), V((G, 8, 256), F32),
            V((G, 8, R), F32), V((G - 1, 8, R), F32),
            V((2, G - 1, 2, B, E), BF16), V((2, G, 2, B, E), BF16), V((2, 4, G, B, E), BF16), V((KC, R), BF16),
            V((4, 4, 32, 2 * R), BF16), V((3, 4, 32, 2 * R), BF16),
            V((4, 8, 128), F32), V((3, 8, 128), F32),
            V((4, 32, 2 * R + 128), F32), V((4, 32, 2 * R + 128), F32), V((3, 32, 2 * R + 128), F32),
            V((4, RC, W), F32), V((2, 3, RC, E), BF16), V((2, 3, RC, E), BF16),
            S(5), S(28), S(28), S(8), S(8), S(8), S(8), S(7), S(7), S(7), S(7),
            S(2, 7), S(2, 7), S(2, 8), S(2, 8), S(2, 8), S(2, 8), S(2, 8), S(2, 8),
            S(3), S(3), S(3), S(3), S(3), S(3), S(3), S(3), S(2, 3), S(2, 3),
        ],
        compiler_params=pltpu.CompilerParams(
            collective_id=0, has_side_effects=True, vmem_limit_bytes=60 * 2**20
        ),
        cost_estimate=pl.CostEstimate(flops=16 * 10**9, bytes_accessed=12 * 10**6, transcendentals=160),
    )(*operands)


def finish_kernel(dense, rg, table, accum, out_u, out_v, out_small, out_rows, out_accum):
    @pl.when(pl.program_id(0) == 0)
    def _():
        out_u[...] = dense[:, pl.ds(0, R)]
        out_v[...] = dense[:, pl.ds(R, R)]
        few = jnp.concatenate([dense[:, pl.ds(2 * R, 128)], jnp.zeros((96, 128), F32)], axis=0).T
        out_small[...] = few[:2, :32]

    n = rg.shape[0]
    for f in range(2):
        g = rg[:, pl.ds(f * E, E)]
        old = jnp.broadcast_to(accum[pl.ds(f, 1), :], (128, n)).T
        new = old + jnp.sum(g * g, axis=1, keepdims=True) * (1.0 / E)
        rows = pl.ds(f, n, stride=2)
        out_rows[rows, :] = table[rows, :] - learn_rate * g / (jnp.sqrt(new) + epsilon)
        out_accum[pl.ds(f, 1), :] = new.T[:1]


def finish(dense, rg, table, accum):
    steps = 4
    n = RC // steps
    whole = lambda *shape: pl.BlockSpec(shape, lambda i: (0, 0))
    return pl.pallas_call(
        finish_kernel,
        grid=(steps,),
        out_shape=(
            jax.ShapeDtypeStruct((32, R), F32),
            jax.ShapeDtypeStruct((32, R), F32),
            jax.ShapeDtypeStruct((2, 32), F32),
            jax.ShapeDtypeStruct((2 * RC, E), F32),
            jax.ShapeDtypeStruct((2, RC), F32),
        ),
        in_specs=[
            whole(32, 2 * R + 128), pl.BlockSpec((n, W), lambda i: (i, 0)),
            pl.BlockSpec((2 * n, E), lambda i: (i, 0)), pl.BlockSpec((2, n), lambda i: (0, i)),
        ],
        out_specs=(
            whole(32, R), whole(32, R), whole(2, 32),
            pl.BlockSpec((2 * n, E), lambda i: (i, 0)), pl.BlockSpec((2, n), lambda i: (0, i)),
        ),
        cost_estimate=pl.CostEstimate(flops=4 * 10**6, bytes_accessed=3 * 2**20, transcendentals=2**18),
    )(dense, rg, table, accum)


def body(
    pooled, cross_v, cross_u, cross_bias, head_weight, labels, fn_weight,
    row_ids, bag_lengths, table_rows, row_accum,
):
    dense, row_grad = fused(
        pooled, cross_v, cross_u, cross_bias[None], head_weight[None], labels[None], fn_weight[None],
        row_ids, bag_lengths,
    )
    grad_u, grad_v, small, rows, accum = finish(dense, row_grad, table_rows.reshape(2 * RC, E), row_accum.T)
    return grad_u.T, grad_v.T, small, rows.reshape(RC, 2, E), accum.T


def solution(mesh):
    placed = (
        P(("hst", "local"), None), P(), P(), P(), P(), P(("hst", "local")), P(("hst", "local")),
        P(None, "hst", None), P("hst", None), P("local", "hst", None), P("local", "hst"),
    )
    both = P(None, ("hst", "local"))
    return jax.shard_map(
        body, mesh=mesh, in_specs=placed,
        out_specs=(both, both, both, P("local", "hst", None), P("local", "hst")),
        check_vma=False,
    )
```

```python
import jax
import jax.numpy as jnp
from jax import lax
from jax.experimental import pallas as pl
from jax.experimental.pallas import tpu as pltpu
from jax.sharding import PartitionSpec as P

learn_rate = 0.05
epsilon = 1e-08
MESH = pl.DeviceIdType.MESH
F32 = jnp.float32
BF16 = jnp.bfloat16

B = 160
R = 512
D = 4096
W = 256
E = 128
G = 8
KC = G * B
RC = 1024
NT = (((1,), (1,)), ((), ()))
TN = (((0,), (0,)), ((), ()))

GROUP = [(2, 0), (2, 1), (1, 0), (3, 0), (1, 1), (3, 1), (0, 1)]
ARRIVE = [(0, 1), (1, 0), (3, 0), (1, 1), (3, 1), (2, 0), (2, 1)]
NEAR = [(0, 0)]
YS = [(0, 1), (1, 0), (1, 1)]
DENSE = [(2, 0), (2, 1), (1, 0), (3, 0), (1, 1), (3, 1), (0, 1)]


def kernel(
    pooled, v_hbm, u_hbm, bias, head, labels, fn_weight, ids_hbm, lens_hbm,
    out_dense, out_rows,
    pool_v, v_v, u_v, scale_v, ids, lens, target, weight, cols_v,
    pool_g, hid_g, low_g, lg_g, small_s, small_g,
    ig_s, e1, gath, half_g,
    dense_s, dense_r, tsmall_s, tsmall_r, d2_s, d2_r, d3_r,
    acc, x_s, x_r,
    loc_sem, pg_s, pg_r, hg_s, hg_r, lo_s, lo_r, lg_s, lg_r, sm_s, sm_r,
    z_s, z_r, y1_s, y1_r, y3_s, y3_r, y2_s, y2_r, dn_s, dn_r, ts_s, ts_r, d2_ss, d2_rs, d3_ss, d3_rs, xs_s, xs_r,
):
    h = lax.axis_index("hst")
    l = lax.axis_index("local")
    z, yh, c = h // 4, (h // 2) % 2, h % 2
    yl, x = l // 4, l % 4
    me = z * 2 + c

    def group_dev(kz, kc):
        zz, cc = (z + kz) % 4, (c + kc) % 2
        return (zz * 4 + yh * 2 + cc, l), zz * 2 + cc

    def y_dev(ka, kb):
        return (z * 4 + ((yh + ka) % 2) * 2 + c, ((yl + kb) % 2) * 4 + x)

    def x_dev(kx):
        return (h, yl * 4 + (x + kx) % 4)

    def dense_dev(kx, kc):
        xx, cc = (x + kx) % 4, (c + kc) % 2
        return (z * 4 + yh * 2 + cc, yl * 4 + xx), xx * 2 + cc

    def dense_cols(m, zt):
        col = (zt * 4 + (m // 4) * 2 + m % 2) * W + ((m // 2) % 2) * E
        return pl.ds(pl.multiple_of(col, E), E)

    def rcopy(src, dst, ss, rs, dev):
        return pltpu.make_async_remote_copy(
            src_ref=src, dst_ref=dst, send_sem=ss, recv_sem=rs, device_id=dev, device_id_type=MESH
        )

    def src_of(kz, kc):
        return ((z - kz + 4) % 4) * 2 + (c + kc) % 2

    barrier = pltpu.get_barrier_semaphore()
    partners = [group_dev(*o)[0] for o in GROUP] + [y_dev(*o) for o in YS] + [dense_dev(*o)[0] for o in DENSE[:-1]]
    for dev in partners:
        pl.semaphore_signal(barrier, inc=1, device_id=dev, device_id_type=MESH)

    def load(src, dst, i):
        cp = pltpu.make_async_copy(src, dst, loc_sem.at[i])
        cp.start()
        return cp

    ld_pool, ld_v, ld_u = load(pooled, pool_v, 2), load(v_hbm, v_v, 3), load(u_hbm, u_v, 4)

    cols_v[...] = jnp.zeros_like(cols_v)
    cols_v[pl.ds(0, 1), pl.ds(0, B)] = labels[...].astype(F32)
    cols_v[pl.ds(1, 1), pl.ds(0, B)] = fn_weight[...].astype(F32)

    def column(row):
        return jnp.broadcast_to(row, (128, row.shape[1])).T

    lab_c = column(cols_v[pl.ds(0, 1), :])[:B]
    fnw_c = column(cols_v[pl.ds(1, 1), :])[:B]

    pl.semaphore_wait(barrier, len(partners))

    sends = []

    def go(copy):
        copy.start()
        sends.append(copy)
        return copy

    pg = []
    for k, (kx, kc) in enumerate(DENSE):
        dev, m = dense_dev(kx, kc)
        for zt in range(4):
            pg.append(go(rcopy(pooled.at[:, dense_cols(m, zt)], pool_g.at[kc * 4 + kx, :, pl.ds(zt * E, E)],
                               pg_s.at[k * 4 + zt], pg_r.at[k * 4 + zt], dev)))

    def spread(buf, ss, rs):
        def far(kx):
            return rcopy(buf.at[0], buf.at[kx], ss.at[kx], rs.at[kx], dense_dev(kx, 0)[0])

        def near(kx):
            return rcopy(buf.at[kx], buf.at[4 + kx], ss.at[4 + kx], rs.at[4 + kx], dense_dev(0, 1)[0])

        for kx in (2, 1, 3):
            far(kx).start()
        near(0).start()

        def relay():
            for kx in (1, 3, 2):
                far(kx).wait_recv()
                near(kx).start()

        def finish():
            for kx in range(4):
                near(kx).wait_recv()

        def drain():
            for kx in range(4):
                near(kx).wait_send()
            for kx in (1, 2, 3):
                far(kx).wait_send()

        return relay, finish, drain

    ld_ids, ld_lens = load(ids_hbm, ids, 0), load(lens_hbm, lens, 1)

    ld_pool.wait()
    ld_v.wait()
    hid_g[0] = lax.dot_general(pool_v[...], v_v[...], NT, preferred_element_type=F32).astype(BF16)
    hid_relay, hid_finish, hid_drain = spread(hid_g, hg_s, hg_r)
    ld_u.wait()

    part = jnp.zeros((B, 128), F32)
    for j in range(8):
        cols = pl.ds(j * 512, 512)
        sc = jnp.dot(hid_g[0], u_v[:, cols], preferred_element_type=F32) + bias[:, cols]
        scale_v[:, cols] = sc
        f = pool_v[:, cols].astype(F32)
        prod = (f * sc + f) * head[:, cols]
        part = part + (prod[:, 0:128] + prod[:, 128:256]) + (prod[:, 256:384] + prod[:, 384:512])
    logits = jnp.sum(part, axis=1, keepdims=True)
    chance = 1.0 / (1.0 + jnp.exp(-jnp.broadcast_to(logits, (B, 128))))
    lgb = fnw_c * (chance - lab_c)
    lg_row = jnp.concatenate([lgb, jnp.zeros((96, 128), F32)], axis=0).T[:8]
    lg_g[0] = lg_row
    lgc = [go(rcopy(lg_g.at[0], lg_g.at[kc * 4 + kx], lg_s.at[k], lg_r.at[k], dense_dev(kx, kc)[0]))
           for k, (kx, kc) in enumerate(DENSE)]
    lgw = jnp.concatenate([lgb, lgb], axis=1)

    low = jnp.zeros((B, R), F32)
    for j in range(16):
        cols = pl.ds(j * W, W)
        f = pool_v[:, cols].astype(F32)
        sg = (lgw * head[:, cols]) * f
        low = low + lax.dot_general(sg.astype(BF16), u_v[:, cols], NT, preferred_element_type=F32)
        mixed = f * scale_v[:, cols] + f
        sums = jnp.concatenate(
            [jnp.sum(sg, axis=0, keepdims=True), jnp.sum(lgw * mixed, axis=0, keepdims=True),
             jnp.zeros((6, W), F32)], axis=0)
        for b in range(2):
            m = (((j // 2) % 2) * 2 + b) * 2 + j % 2
            small_s[m, :, pl.ds((j // 4) * E, E)] = sums[:, b * E:(b + 1) * E]
    low_g[0] = low.astype(BF16)
    low_relay, low_finish, low_drain = spread(low_g, lo_s, lo_r)

    def z_copy(f, k, dev):
        return rcopy(ig_s.at[f, k], e1.at[f, me], z_s.at[f, k], z_r.at[f, k], dev)

    for k, off in enumerate(GROUP + [(0, 0)]):
        dev, m = group_dev(*off)
        for b in range(2):
            cols = pl.ds(pl.multiple_of(((m // 2) * 4 + b * 2 + m % 2) * W, W), W)
            ig = ((lgw * head[:, cols]) * (scale_v[:, cols] + 1.0) + jnp.dot(
                low_g[0], v_v[:, cols], preferred_element_type=F32)).astype(BF16)
            for f in range(2):
                if k < 7:
                    ig_s[f, k, b] = ig[:, f * E:(f + 1) * E]
                else:
                    e1[f, me, b] = ig[:, f * E:(f + 1) * E]
        if k < 7:
            go(z_copy(0, k, dev))
    smc = []
    for k, (kx, kc) in enumerate(DENSE):
        dev, m = dense_dev(kx, kc)
        smc.append(go(rcopy(small_s.at[m], small_g.at[k], sm_s.at[k], sm_r.at[k], dev)))

    def y1_copy(f, m):
        return rcopy(e1.at[f, m, yh], gath.at[f, 1, m], y1_s.at[f, m], y1_r.at[f, m], y_dev(0, 1))

    def y3_copy(f, m):
        return rcopy(e1.at[f, m, 1 - yh], gath.at[f, 3, m], y3_s.at[f, m], y3_r.at[f, m], y_dev(1, 1))

    def y2_copy(f, m):
        return rcopy(gath.at[f, 3, m], gath.at[f, 2, m], y2_s.at[f, m], y2_r.at[f, m], y_dev(0, 1))

    def forward(f, m):
        y3_copy(f, m).start()
        y1_copy(f, m).start()
        gath[f, 0, m] = e1[f, m, yh]

    def forward_all(f, order):
        for kz, kc in order:
            z_copy(f, GROUP.index((kz, kc)), (h, l)).wait_recv()
            forward(f, src_of(kz, kc))

    def relay_all(f, order):
        for kz, kc in order:
            m = src_of(kz, kc)
            y3_copy(f, m).wait_recv()
            y2_copy(f, m).start()

    forward(0, me)
    forward_all(0, ARRIVE[:1])
    forward(1, me)

    ld_ids.wait()
    ld_lens.wait()
    lane = lax.broadcasted_iota(jnp.int32, (8, 640), 1)
    for ys in range(4):
        for g in range(2):
            out = jnp.zeros((8, 640), jnp.int32)
            for i in range(4):
                hs = (2 * g + i // 2) * 4 + (ys // 2) * 2 + i % 2
                win = pl.ds(hs * 1280 + (ys % 2) * 640, 640)
                ln = lens[:, win]
                got = jnp.concatenate([jnp.where(ln > s, ids[s, :, win], -1) for s in range(4)], axis=0)
                got = pltpu.roll(got, (160 * i + 640 - 160 * x) % 640, 1)
                out = jnp.where((lane >= 160 * i) & (lane < 160 * (i + 1)), got, out)
            target[:, pl.ds((ys * 2 + g) * 640, 640)] = out.astype(F32)
    for f in range(2):
        t = [target[pl.ds(s * 2 + f, 1), :] for s in range(4)]
        e01, e02, e03 = t[0] == t[1], t[0] == t[2], t[0] == t[3]
        e12, e13, e23 = t[1] == t[2], t[1] == t[3], t[2] == t[3]
        one = lambda m: jnp.where(m, 1.0, 0.0)
        weight[pl.ds(f, 1), :] = 1.0 + one(e01) + one(e02) + one(e03)
        weight[pl.ds(2 + f, 1), :] = 1.0 + one(e12) + one(e13)
        weight[pl.ds(4 + f, 1), :] = 1.0 + one(e23)
        weight[pl.ds(6 + f, 1), :] = jnp.ones_like(t[0])
        target[pl.ds(2 + f, 1), :] = jnp.where(e01, -1.0, t[1])
        target[pl.ds(4 + f, 1), :] = jnp.where(e02 | e12, -1.0, t[2])
        target[pl.ds(6 + f, 1), :] = jnp.where(e03 | e13 | e23, -1.0, t[3])

    forward_all(0, ARRIVE[1:])
    for k, off in enumerate(GROUP):
        go(z_copy(1, k, group_dev(*off)[0]))
    acc[...] = jnp.zeros_like(acc)

    def d1_copies(k):
        kz = (2, 1, 3)[k]
        dev, zz = group_dev(kz, 0)[0], (z + kz) % 4
        return (rcopy(dense_s.at[zz], dense_r.at[k], dn_s.at[k], dn_r.at[k], dev),
                rcopy(tsmall_s.at[zz], tsmall_r.at[k], ts_s.at[k], ts_r.at[k], dev))

    def dense_products():
        mine = x * 2 + c
        own_cols = [dense_cols(mine, zt) for zt in range(4)]
        for zt in range(4):
            pool_g[0, :, pl.ds(zt * E, E)] = pool_v[:, own_cols[zt]]
        own_head = jnp.concatenate([head[:, own_cols[zt]] for zt in range(4)], axis=1)

        for cp in pg + lgc:
            cp.wait_recv()
        hid_finish()
        for k in range(8):
            lgk = jnp.concatenate([lg_g[k]] * 16, axis=0).T[:B]
            lgk = jnp.concatenate([lgk] * 4, axis=1)
            half_g[pl.ds(k * B, B), :] = ((lgk * own_head) * pool_g[k].astype(F32)).astype(BF16)
        dense_s[:, :, :, pl.ds(0, R)] = lax.dot_general(
            half_g[...], hid_g[...].reshape(KC, R), TN, preferred_element_type=F32
        ).astype(BF16).reshape(4, 4, 32, R)
        low_finish()
        for cp in smc:
            cp.wait_recv()
        dense_s[:, :, :, pl.ds(R, R)] = lax.dot_general(
            pool_g[...].reshape(KC, R), low_g[...].reshape(KC, R), TN, preferred_element_type=F32
        ).astype(BF16).reshape(4, 4, 32, R)
        tot = small_s[mine]
        for k in range(7):
            tot = tot + small_g[k]
        for zt in range(4):
            tsmall_s[zt] = tot[:, zt * E:(zt + 1) * E]
        for k in range(3):
            for cp in d1_copies(k):
                cp.start()

    iota = lax.broadcasted_iota(jnp.int32, (16, KC), 0).astype(F32).astype(BF16)

    def x_off(kx):
        return (2 - kx + (kx // 2) * 3 + (kx // 3) * 2) % 4

    def x_copy(f, kx):
        return rcopy(x_s.at[f, kx], x_r.at[f, kx], xs_s.at[f, kx], xs_r.at[f, kx], x_dev(x_off(kx)))

    def d2_copy(k):
        xx = (x + k + 1) % 4
        return rcopy(d2_s.at[xx], d2_r.at[x], d2_ss.at[k], d2_rs.at[k], x_dev(k + 1))

    def d3_copy(k):
        ka, kb = YS[k]
        yy = ((yh + ka) % 2) * 2 + (yl + kb) % 2
        return rcopy(d2_r.at[yy], d3_r.at[k], d3_ss.at[k], d3_rs.at[k], y_dev(ka, kb))

    def row_sums(f):
        for kx in range(3):
            x_copy(f, kx).wait_recv()
        out_rows[:, pl.ds(f * E, E)] = (
            acc[3, :, pl.ds(f * E, E)] + (x_r[f, 0].astype(F32) + x_r[f, 1].astype(F32)) + x_r[f, 2].astype(F32))

    def wait_y(copy, f):
        def one(m, cc):
            copy(f, m).wait_recv()
            return cc
        lax.fori_loop(0, 8, one, 0)

    def sum_along_z():
        for k in range(3):
            for cp in d1_copies(k):
                cp.wait_recv()
        d2_s[:, :, pl.ds(0, 2 * R)] = (
            (dense_s[z].astype(F32) + dense_r[0].astype(F32))
            + (dense_r[1].astype(F32) + dense_r[2].astype(F32)))
        few = (tsmall_s[z] + tsmall_r[0]) + (tsmall_r[1] + tsmall_r[2])
        d2_s[:, :, pl.ds(2 * R, 128)] = jnp.concatenate(
            [few, jnp.zeros((120, 128), F32)], axis=0).T.reshape(4, 32, 128)
        d2_r[x] = d2_s[x]
        for k in range(3):
            d2_copy(k).start()

    def blocks_along_y():
        for k in range(3):
            d2_copy(k).wait_recv()
        for k in range(3):
            d3_copy(k).start()

    def at(t, when, act):
        pl.when(t == when)(act)

    def step(t, carry):
        late = t // 24
        s = (1 - late) * (t // 4) + late * (6 + t % 2)
        kx = (1 - late) * (t % 4) + late * ((t - 24) // 2)
        f, dd = s // 4, s % 4
        d = dd + (dd // 2) * (1 - 2 * (dd % 2))
        at(t, 1, lambda: relay_all(0, NEAR + ARRIVE))
        at(t, 4, lambda: wait_y(y1_copy, 0))
        at(t, 7, lambda: forward_all(1, ARRIVE))
        at(t, 10, hid_relay)
        at(t, 11, lambda: relay_all(1, NEAR + ARRIVE[:3]))
        at(t, 12, lambda: wait_y(y2_copy, 0))
        at(t, 12, low_relay)
        at(t, 13, dense_products)
        at(t, 15, lambda: relay_all(1, ARRIVE[3:]))
        at(t, 20, lambda: wait_y(y1_copy, 1))
        at(t, 24, sum_along_z)
        at(t, 24, lambda: wait_y(y2_copy, 1))
        at(t, 30, blocks_along_y)
        at(t, 30, lambda: row_sums(0))

        src = ((yh + d // 2) % 2) * 2 + (yl + d % 2) % 2
        lanes = pl.ds(pl.multiple_of(src * KC, 128), KC)
        fcols = pl.ds(pl.multiple_of(f * E, E), E)

        base = (yl * 4 + (x + x_off(kx)) % 4) * RC
        tt = [target[pl.ds(q * 2 + f, 1), lanes] for q in range(4)]
        ws = [jnp.broadcast_to(weight[pl.ds(q * 2 + f, 1), lanes], (16, KC)).astype(BF16)
              for q in range(4)]
        tiles = []
        for sb in range(RC // 256):
            low_row = (base + sb * 256).astype(F32)
            ts = [jnp.broadcast_to(tt[q] - low_row, (16, KC)).astype(BF16) for q in range(4)]
            for i in range(16):
                it = iota + jnp.asarray(16 * i, BF16)
                cnt = jnp.zeros((16, KC), BF16)
                for q in range(4):
                    cnt = jnp.where(it == ts[q], ws[q], cnt)
                tiles.append(cnt)
        counts = jnp.concatenate(tiles, axis=0)
        g = gath[f, d].reshape(KC, E)
        acc[kx, :, fcols] += jnp.dot(counts, g, preferred_element_type=F32)

        @pl.when((dd == 3) & (kx < 3))
        def _():
            x_s[f, kx] = acc[kx, :, fcols].astype(BF16)
            x_copy(f, kx).start()
        return carry

    lax.fori_loop(0, 32, step, 0)

    for k in range(3):
        d3_copy(k).wait_recv()
    out_dense[...] = (d2_r[yh * 2 + yl] + d3_r[0]) + (d3_r[1] + d3_r[2])
    row_sums(1)

    for f in range(2):
        for kx in range(3):
            x_copy(f, kx).wait_send()

        def drain(m, cc):
            y1_copy(f, m).wait_send()
            y3_copy(f, m).wait_send()
            y2_copy(f, m).wait_send()
            return cc
        lax.fori_loop(0, 8, drain, 0)
    for k in range(3):
        d2_copy(k).wait_send()
        d3_copy(k).wait_send()
        for cp in d1_copies(k):
            cp.wait_send()
    hid_drain()
    low_drain()
    for cp in sends:
        cp.wait_send()


def fused(*operands):
    any_, vmem = pl.BlockSpec(memory_space=pl.ANY), pl.BlockSpec(memory_space=pltpu.VMEM)
    V, S = pltpu.VMEM, lambda *n: pltpu.SemaphoreType.DMA(n)
    return pl.pallas_call(
        kernel,
        out_shape=(jax.ShapeDtypeStruct((32, 2 * R + 128), F32), jax.ShapeDtypeStruct((RC, W), F32)),
        in_specs=[any_, any_, any_, vmem, vmem, vmem, vmem, any_, any_],
        out_specs=(vmem, vmem),
        scratch_shapes=[
            V((B, D), BF16), V((R, D), BF16), V((R, D), BF16), V((B, D), F32),
            V((4, 2, 20480), jnp.int32), V((2, 20480), jnp.int32),
            V((8, 4 * KC), F32), V((8, 4 * KC), F32), V((8, 256), F32),
            V((G, B, R), BF16), V((G, B, R), BF16), V((G, B, R), BF16), V((G, 8, 256), F32),
            V((G, 8, R), F32), V((G - 1, 8, R), F32),
            V((2, G - 1, 2, B, E), BF16), V((2, G, 2, B, E), BF16), V((2, 4, G, B, E), BF16), V((KC, R), BF16),
            V((4, 4, 32, 2 * R), BF16), V((3, 4, 32, 2 * R), BF16),
            V((4, 8, 128), F32), V((3, 8, 128), F32),
            V((4, 32, 2 * R + 128), F32), V((4, 32, 2 * R + 128), F32), V((3, 32, 2 * R + 128), F32),
            V((4, RC, W), F32), V((2, 3, RC, E), BF16), V((2, 3, RC, E), BF16),
            S(5), S(28), S(28), S(8), S(8), S(8), S(8), S(7), S(7), S(7), S(7),
            S(2, 7), S(2, 7), S(2, 8), S(2, 8), S(2, 8), S(2, 8), S(2, 8), S(2, 8),
            S(3), S(3), S(3), S(3), S(3), S(3), S(3), S(3), S(2, 3), S(2, 3),
        ],
        compiler_params=pltpu.CompilerParams(
            collective_id=0, has_side_effects=True, vmem_limit_bytes=60 * 2**20
        ),
        cost_estimate=pl.CostEstimate(flops=16 * 10**9, bytes_accessed=12 * 10**6, transcendentals=160),
    )(*operands)


def finish_kernel(dense, rg, table, accum, out_u, out_v, out_small, out_rows, out_accum):
    @pl.when(pl.program_id(0) == 0)
    def _():
        out_u[...] = dense[:, pl.ds(0, R)]
        out_v[...] = dense[:, pl.ds(R, R)]
        few = jnp.concatenate([dense[:, pl.ds(2 * R, 128)], jnp.zeros((96, 128), F32)], axis=0).T
        out_small[...] = few[:2, :32]

    n = rg.shape[0]
    for f in range(2):
        g = rg[:, pl.ds(f * E, E)]
        old = jnp.broadcast_to(accum[pl.ds(f, 1), :], (128, n)).T
        new = old + jnp.sum(g * g, axis=1, keepdims=True) * (1.0 / E)
        rows = pl.ds(f, n, stride=2)
        out_rows[rows, :] = table[rows, :] - learn_rate * g / (jnp.sqrt(new) + epsilon)
        out_accum[pl.ds(f, 1), :] = new.T[:1]


def finish(dense, rg, table, accum):
    steps = 2
    n = RC // steps
    whole = lambda *shape: pl.BlockSpec(shape, lambda i: (0, 0))
    return pl.pallas_call(
        finish_kernel,
        grid=(steps,),
        out_shape=(
            jax.ShapeDtypeStruct((32, R), F32),
            jax.ShapeDtypeStruct((32, R), F32),
            jax.ShapeDtypeStruct((2, 32), F32),
            jax.ShapeDtypeStruct((2 * RC, E), F32),
            jax.ShapeDtypeStruct((2, RC), F32),
        ),
        in_specs=[
            whole(32, 2 * R + 128), pl.BlockSpec((n, W), lambda i: (i, 0)),
            pl.BlockSpec((2 * n, E), lambda i: (i, 0)), pl.BlockSpec((2, n), lambda i: (0, i)),
        ],
        out_specs=(
            whole(32, R), whole(32, R), whole(2, 32),
            pl.BlockSpec((2 * n, E), lambda i: (i, 0)), pl.BlockSpec((2, n), lambda i: (0, i)),
        ),
        cost_estimate=pl.CostEstimate(flops=4 * 10**6, bytes_accessed=3 * 2**20, transcendentals=2**18),
    )(dense, rg, table, accum)


def body(
    pooled, cross_v, cross_u, cross_bias, head_weight, labels, fn_weight,
    row_ids, bag_lengths, table_rows, row_accum,
):
    dense, row_grad = fused(
        pooled, cross_v, cross_u, cross_bias[None], head_weight[None], labels[None], fn_weight[None],
        row_ids, bag_lengths,
    )
    grad_u, grad_v, small, rows, accum = finish(dense, row_grad, table_rows.reshape(2 * RC, E), row_accum.T)
    return grad_u.T, grad_v.T, small, rows.reshape(RC, 2, E), accum.T


def solution(mesh):
    placed = (
        P(("hst", "local"), None), P(), P(), P(), P(), P(("hst", "local")), P(("hst", "local")),
        P(None, "hst", None), P("hst", None), P("local", "hst", None), P("local", "hst"),
    )
    both = P(None, ("hst", "local"))
    return jax.shard_map(
        body, mesh=mesh, in_specs=placed,
        out_specs=(both, both, both, P("local", "hst", None), P("local", "hst")),
        check_vma=False,
    )
```
